32 devices in a mesh: frame: 8 (over z, y), tensor: 2 (over x), dp: 2 (over core).
Axes of the slice: x: 2, y: 2, z: 4, core: 2. Of those that a mesh axis runs over, the one named last changes fastest.
Arguments:
- q_proj: bfloat16 [8192, 768], P(('dp', 'frame'), 'tensor'), parts along dimension 0
- k_proj: bfloat16 [8192, 768], P(('dp', 'frame'), 'tensor'), parts along dimension 0
- v_proj: bfloat16 [8192, 768], P(('dp', 'frame'), 'tensor'), parts along dimension 0, may hold values from -6 to 6
- gain_q: float32 [768], P('tensor'), may hold values from 0.5 to 6
- gain_k: float32 [768], P('tensor'), may hold values from 0.5 to 6
- tiles: int32 [64, 12], P('dp'), parts along dimension 0, may hold values from 0 to 31, as said below
Outputs:
- attended: bfloat16 [8192, 768], P(('dp', 'frame'), 'tensor'), parts along dimension 0
The draws below stay inside these ranges and needn't reach their ends.
There are 2 independent parts, one for each index of `dp`. The reference program is written for one: setup_inputs(seed, part) draws one part's arguments, and reference() takes and returns one part's arrays. A program takes and returns all parts, laid end to end along the dimension named above; an argument that names none is the same for every part. Nothing has to cross between parts.
Inputs may be any that keep to these rules, and one draw needn't show every extreme that they name: `tiles`: row q lists 12 distinct key blocks: q first; then 8 blocks whose slab (group of 4 consecutive blocks, one frame slab) is at most 2 slabs from the slab of q; then 3 blocks that are each the first block of a slab more than 2 slabs away. Farther groups are listed less often.
All inputs are finite; a program needn't handle non-finite values.
Results may differ from the reference program's by a relative error of at most 0.007.
The reference program's roundings to bfloat16 on the way count: a program that leaves them out, or rounds other values in their place, can miss the bound.
Values may be sent and summed in bfloat16 or wider, within the bound.
A program may use at most 128 MiB of HBM per device.

```python
import math
import jax
import jax.numpy as jnp
from jax import lax

HD = 128
BLK = 128
NEAR = 2
FAR_SLOTS = 3
KSLOTS = 12
TOK_DEV = 512
TOKENS = 4096
NBLK = 32
HEADS = 6


def draw_pair(key):
    width = HEADS * HD
    col_pos = jnp.arange(width, dtype=jnp.float32) / (width - 1)
    rising = 3.0 ** (0.5 * col_pos)
    log_ten = math.log(10.0)

    def scaled(salt):
        noise = jax.random.truncated_normal(jax.random.fold_in(key, salt), -5.0, 5.0, (TOKENS, width), jnp.float32)
        row_scale = jnp.exp(jax.random.uniform(jax.random.fold_in(key, salt + 1), (TOKENS, 1), jnp.float32) * log_ten)
        col_scale = jnp.exp(jax.random.uniform(jax.random.fold_in(key, salt + 2), (1, width), jnp.float32) * log_ten)
        return noise * row_scale * col_scale * rising
    query = scaled(301)
    keyed = scaled(401)
    return (query, keyed)


def draw_q_proj(key, part):
    return draw_pair(key)[0].astype(jnp.bfloat16)


def draw_k_proj(key, part):
    return draw_pair(key)[1].astype(jnp.bfloat16)


def draw_gain(key):
    width = HEADS * HD
    return jnp.exp(jax.random.uniform(key, (width,), jnp.float32, math.log(0.5), math.log(2.0)))


def draw_gain_q(key, part):
    return draw_gain(jax.random.fold_in(key, 11))


def draw_gain_k(key, part):
    return draw_gain(jax.random.fold_in(key, 13))


def draw_tiles(key, part):
    block_count = NBLK
    per_slab = TOK_DEV // BLK
    index = jnp.arange(block_count, dtype=jnp.int32)
    slab = index // per_slab
    distance = jnp.abs(slab[:, None] - slab[None, :])
    near_ok = (distance <= NEAR) & (index[:, None] != index[None, :])
    far_ok = (distance > NEAR) & (index % per_slab == 0)[None, :]
    raw = jax.random.randint(jax.random.fold_in(key, 21), (block_count, block_count), 0, 4096, jnp.int32)
    score = raw // (1 + distance) * block_count + index[None, :]
    near_score = jnp.where(near_ok, score, -1)
    far_score = jnp.where(far_ok, score, -1)
    near_pick = lax.top_k(near_score, KSLOTS - 1 - FAR_SLOTS)[1].astype(jnp.int32)
    far_pick = lax.top_k(far_score, FAR_SLOTS)[1].astype(jnp.int32)
    return jnp.concatenate([index[:, None], near_pick, far_pick], axis=1).astype(jnp.int32)


def levels(key, dims, pieces, smallest, high):
    level = 1.0
    for position, parts in pieces:
        steps = jax.random.uniform(jax.random.fold_in(jax.random.fold_in(key, 6), position), (parts,), jnp.float32, smallest / len(pieces), high / len(pieces))
        level = level * jnp.repeat(jnp.exp(steps), dims[position] // parts).reshape((-1,) + (1,) * (len(dims) - 1 - position))
    return level


def bell_draw(key, shape, scale, reach, cuts=(), kind=jnp.bfloat16):
    array = jax.random.normal(key, shape, jnp.float32) * scale
    if len(cuts) > 0:
        array = levels(key, shape, cuts, -0.22, 0.18) * array
    return jnp.clip(array, min=-reach, max=reach).astype(kind)


def setup_inputs(seed: int = 0, part: int = 0) -> dict:
    streams_of = jax.random.split(jax.random.key(seed), 7)
    own_keys = jax.random.split(jax.random.fold_in(streams_of[6], part), 7)
    return {
        "q_proj": draw_q_proj(jax.random.fold_in(jax.random.fold_in(streams_of[6], part), 71), part),
        "k_proj": draw_k_proj(jax.random.fold_in(jax.random.fold_in(streams_of[6], part), 71), part),
        "v_proj": bell_draw(own_keys[2], (TOKENS, HEADS * HD), 1.0, 6.0, ((0, 8), (1, 2))),
        "gain_q": draw_gain_q(jax.random.fold_in(streams_of[6], 71), part),
        "gain_k": draw_gain_k(jax.random.fold_in(streams_of[6], 71), part),
        "tiles": draw_tiles(jax.random.fold_in(jax.random.fold_in(streams_of[6], part), 71), part),
    }


EPS = 1e-06

def normed(values, gain):
    wide = values.astype(jnp.float32)
    mean_sq = lax.optimization_barrier(jnp.sum(wide * wide, axis=1, keepdims=True)) / wide.shape[1]
    return (wide * lax.rsqrt(mean_sq + EPS) * gain).astype(jnp.bfloat16)

def reference(q_proj, k_proj, v_proj, gain_q, gain_k, tiles):
    width = q_proj.shape[1]
    q_norm = normed(q_proj, gain_q)
    k_norm = normed(k_proj, gain_k)
    q_blocks = q_norm.reshape(NBLK, BLK, HEADS, HD)
    k_blocks = k_norm.reshape(NBLK, BLK, HEADS, HD)
    v_blocks = v_proj.reshape(NBLK, BLK, HEADS, HD)
    scale = 1.0 / math.sqrt(HD)

    def one_block(inputs):
        q_block, listed = inputs
        keys = k_blocks[listed].reshape(KSLOTS * BLK, HEADS, HD)
        values = v_blocks[listed].reshape(KSLOTS * BLK, HEADS, HD)
        scores = jnp.einsum('qhd,khd->hqk', q_block.astype(jnp.float32), keys.astype(jnp.float32)) * scale
        top = lax.optimization_barrier(jnp.max(scores, axis=-1, keepdims=True))
        weights = jnp.exp(scores - top)
        totals = lax.optimization_barrier(jnp.sum(weights, axis=-1))
        rounded = lax.optimization_barrier(weights.astype(jnp.bfloat16))
        summed = jnp.einsum('hqk,khd->hqd', rounded.astype(jnp.float32), values.astype(jnp.float32))
        result = summed / totals[..., None]
        return jnp.transpose(result, (1, 0, 2)).reshape(BLK, width).astype(jnp.bfloat16)
    outputs = lax.map(one_block, (q_blocks, tiles))
    return outputs.reshape(TOKENS, width)
```

```python
import functools
import math

import jax
import jax.numpy as jnp
from jax import lax
from jax.experimental import pallas as pl
from jax.experimental.pallas import tpu as pltpu
from jax.sharding import PartitionSpec as P

HD = 128
BLK = 128
NEAR = 2
EPS = 1e-06
MASKED = -1e30
MESH = pl.DeviceIdType.MESH


def kernel(
    frames,
    tensors,
    tiles_ref,
    q_ref,
    k_ref,
    v_ref,
    gq_ref,
    gk_ref,
    out_ref,
    kbuf,
    vbuf,
    qn,
    sums,
    listed,
    acc_ref,
    max_ref,
    sum_ref,
    send_k,
    send_v,
    recv_k,
    recv_v,
    send_s,
    recv_s,
):
    me = lax.axis_index("frame")
    tpos = lax.axis_index("tensor")
    rows, width = q_ref.shape
    heads = width // HD
    blocks = rows // BLK
    slots = tiles_ref.shape[1]

    barrier = pltpu.get_barrier_semaphore()
    for step in range(1, frames):
        pl.semaphore_signal(
            barrier, inc=1, device_id={"frame": lax.rem(me + step, frames)}, device_id_type=MESH
        )
    for step in range(1, tensors):
        pl.semaphore_signal(
            barrier, inc=1, device_id={"tensor": lax.rem(tpos + step, tensors)}, device_id_type=MESH
        )
    pl.semaphore_wait(barrier, frames - 1 + tensors - 1)

    def full_copy(src, buf, send, recv, dest):
        return pltpu.make_async_remote_copy(
            src_ref=src,
            dst_ref=buf.at[me],
            send_sem=send.at[dest],
            recv_sem=recv.at[me],
            device_id={"frame": dest},
            device_id_type=MESH,
        )

    def first_copy(src, buf, send, recv, dest):
        return pltpu.make_async_remote_copy(
            src_ref=src.at[pl.ds(0, BLK)],
            dst_ref=buf.at[me, pl.ds(0, BLK)],
            send_sem=send.at[dest],
            recv_sem=recv.at[me],
            device_id={"frame": dest},
            device_id_type=MESH,
        )

    side = 1 - 2 * lax.rem(me, 2)
    order = (me + side, me + 2, me - 2, me - side)

    def each_near(action):
        for other in order:

            @pl.when(jnp.logical_and(other >= 0, other < frames))
            def _():
                action(other)

    def each_far(action):
        @pl.loop(0, frames)
        def _(other):
            @pl.when(jnp.abs(other - me) > NEAR)
            def _():
                action(other)

    each_near(lambda dest: full_copy(v_ref, vbuf, send_v, recv_v, dest).start())

    def squares(ref):
        total = None
        for head in range(heads):
            wide = ref[:, head * HD : (head + 1) * HD].astype(jnp.float32)
            total = wide * wide if total is None else total + wide * wide
        return jnp.sum(jnp.transpose(total), axis=0, keepdims=True)

    sums[tpos] = jnp.concatenate(
        [squares(q_ref), squares(k_ref), jnp.zeros((6, rows), jnp.float32)], axis=0
    )

    def sums_copy(peer):
        return pltpu.make_async_remote_copy(
            src_ref=sums.at[tpos],
            dst_ref=sums.at[tpos],
            send_sem=send_s.at[peer],
            recv_sem=recv_s.at[tpos],
            device_id={"tensor": peer},
            device_id_type=MESH,
        )

    for step in range(1, tensors):
        sums_copy(lax.rem(tpos + step, tensors)).start()

    each_far(lambda dest: first_copy(v_ref, vbuf, send_v, recv_v, dest).start())

    for slot in range(slots):
        listed[slot : slot + 1, :] = jnp.concatenate(
            [
                jnp.full((1, BLK), tiles_ref[me * blocks + block, slot], jnp.int32)
                for block in range(blocks)
            ],
            axis=1,
        )

    for step in range(1, tensors):
        peer = lax.rem(tpos + step, tensors)
        pltpu.make_async_copy(sums.at[peer], sums.at[peer], recv_s.at[peer]).wait()
    total = sums[0]
    for other in range(1, tensors):
        total = total + sums[other]
    factor = lax.rsqrt(total / (width * tensors) + EPS)

    def normed(ref, row, gain, store):
        scale = jnp.transpose(jnp.broadcast_to(factor[row : row + 1], (HD, rows)))
        for head in range(heads):
            columns = slice(head * HD, (head + 1) * HD)
            wide = ref[:, columns].astype(jnp.float32)
            store(columns, (wide * scale * gain[:, columns]).astype(jnp.bfloat16))

    def store_k(columns, value):
        kbuf[me, :, columns] = value

    def store_q(columns, value):
        qn[:, columns] = value

    normed(k_ref, 1, gk_ref, store_k)
    each_near(lambda dest: full_copy(kbuf.at[me], kbuf, send_k, recv_k, dest).start())
    each_far(lambda dest: first_copy(kbuf.at[me], kbuf, send_k, recv_k, dest).start())
    normed(q_ref, 0, gq_ref, store_q)

    acc_ref[...] = jnp.zeros_like(acc_ref)
    max_ref[...] = jnp.full_like(max_ref, MASKED)
    sum_ref[...] = jnp.zeros_like(sum_ref)
    to_exponent = math.log2(math.e) / math.sqrt(HD)

    def attend(slab, keys, values):
        count = keys.shape[0] // BLK
        biases = []
        for block in range(count):
            hit = jnp.any(listed[0:slots, :] == slab * blocks + block, axis=0, keepdims=True)
            biases.append(jnp.where(hit, 0.0, MASKED))
        for head in range(heads):
            columns = slice(head * HD, (head + 1) * HD)
            scores = lax.dot_general(
                keys[:, columns],
                qn[:, columns],
                (((1,), (1,)), ((), ())),
                preferred_element_type=jnp.float32,
            )
            parts = [
                scores[block * BLK : (block + 1) * BLK] * to_exponent + biases[block]
                for block in range(count)
            ]
            top = functools.reduce(jnp.maximum, parts)
            old_max = max_ref[head : head + 1, :]
            new_max = jnp.maximum(old_max, jnp.max(top, axis=0, keepdims=True))
            shrink = jnp.exp2(old_max - new_max)
            weights = [jnp.exp2(part - new_max) for part in parts]
            added = functools.reduce(jnp.add, weights)
            max_ref[head : head + 1, :] = new_max
            sum_ref[head : head + 1, :] = sum_ref[head : head + 1, :] * shrink + jnp.sum(
                added, axis=0, keepdims=True
            )
            rounded = jnp.concatenate([weight.astype(jnp.bfloat16) for weight in weights], axis=0)
            product = lax.dot_general(
                values[:, columns],
                rounded,
                (((0,), (0,)), ((), ())),
                preferred_element_type=jnp.float32,
            )
            acc_ref[head] = acc_ref[head] * shrink + product

    attend(me, kbuf.at[me], v_ref)

    def near_step(other):
        pltpu.make_async_copy(vbuf.at[other], vbuf.at[other], recv_v.at[other]).wait()
        pltpu.make_async_copy(kbuf.at[other], kbuf.at[other], recv_k.at[other]).wait()
        attend(other, kbuf.at[other], vbuf.at[other])

    each_near(near_step)

    def far_step(other):
        piece_v = vbuf.at[other, pl.ds(0, BLK)]
        piece_k = kbuf.at[other, pl.ds(0, BLK)]
        pltpu.make_async_copy(piece_v, piece_v, recv_v.at[other]).wait()
        pltpu.make_async_copy(piece_k, piece_k, recv_k.at[other]).wait()
        attend(other, piece_k, piece_v)

    each_far(far_step)

    for head in range(heads):
        value = acc_ref[head] / sum_ref[head : head + 1, :]
        out_ref[:, head * HD : (head + 1) * HD] = jnp.transpose(value).astype(jnp.bfloat16)

    each_near(lambda dest: full_copy(v_ref, vbuf, send_v, recv_v, dest).wait_send())
    each_near(lambda dest: full_copy(kbuf.at[me], kbuf, send_k, recv_k, dest).wait_send())
    each_far(lambda dest: first_copy(v_ref, vbuf, send_v, recv_v, dest).wait_send())
    each_far(lambda dest: first_copy(kbuf.at[me], kbuf, send_k, recv_k, dest).wait_send())
    for step in range(1, tensors):
        sums_copy(lax.rem(tpos + step, tensors)).wait_send()


def body(frames, tensors, q_proj, k_proj, v_proj, gain_q, gain_k, tiles):
    rows, width = q_proj.shape
    heads = width // HD
    vmem = pl.BlockSpec(memory_space=pltpu.VMEM)
    slots = -(-tiles.shape[1] // 8) * 8
    return pl.pallas_call(
        functools.partial(kernel, frames, tensors),
        out_shape=jax.ShapeDtypeStruct((rows, width), jnp.bfloat16),
        in_specs=[pl.BlockSpec(memory_space=pltpu.SMEM)] + [vmem] * 5,
        out_specs=vmem,
        scratch_shapes=[
            pltpu.VMEM((frames, rows, width), jnp.bfloat16),
            pltpu.VMEM((frames, rows, width), jnp.bfloat16),
            pltpu.VMEM((rows, width), jnp.bfloat16),
            pltpu.VMEM((tensors, 8, rows), jnp.float32),
            pltpu.VMEM((slots, rows), jnp.int32),
            pltpu.VMEM((heads, HD, rows), jnp.float32),
            pltpu.VMEM((8, rows), jnp.float32),
            pltpu.VMEM((8, rows), jnp.float32),
            pltpu.SemaphoreType.DMA((frames,)),
            pltpu.SemaphoreType.DMA((frames,)),
            pltpu.SemaphoreType.DMA((frames,)),
            pltpu.SemaphoreType.DMA((frames,)),
            pltpu.SemaphoreType.DMA((tensors,)),
            pltpu.SemaphoreType.DMA((tensors,)),
        ],
        compiler_params=pltpu.CompilerParams(
            collective_id=0, has_side_effects=True, vmem_limit_bytes=40 * 1024 * 1024
        ),
    )(tiles, q_proj, k_proj, v_proj, gain_q.reshape(1, width), gain_k.reshape(1, width))


def solution(mesh):
    return jax.shard_map(
        functools.partial(body, mesh.shape["frame"], mesh.shape["tensor"]),
        mesh=mesh,
        in_specs=(
            P(("dp", "frame"), "tensor"),
            P(("dp", "frame"), "tensor"),
            P(("dp", "frame"), "tensor"),
            P("tensor"),
            P("tensor"),
            P("dp", None),
        ),
        out_specs=P(("dp", "frame"), "tensor"),
        check_vma=False,
    )
```

```python
import functools
import math

import jax
import jax.numpy as jnp
from jax import lax
from jax.experimental import pallas as pl
from jax.experimental.pallas import tpu as pltpu
from jax.sharding import PartitionSpec as P

HD = 128
BLK = 128
NEAR = 2
EPS = 1e-06
MASKED = -1e30
MESH = pl.DeviceIdType.MESH


def kernel(
    frames,
    tensors,
    tiles_hbm,
    q_hbm,
    k_hbm,
    v_hbm,
    gq_hbm,
    gk_hbm,
    out_ref,
    tiles_ref,
    q_ref,
    k_ref,
    gq_ref,
    gk_ref,
    kbuf,
    vbuf,
    qn,
    sums,
    listed,
    acc_ref,
    max_ref,
    sum_ref,
    load_sem,
    send_k,
    send_v,
    recv_k,
    recv_v,
    send_s,
    recv_s,
):
    me = lax.axis_index("frame")
    tpos = lax.axis_index("tensor")
    rows, width = q_ref.shape
    heads = width // HD
    blocks = rows // BLK
    slots = tiles_ref.shape[1]
    half = rows // 2

    loads = [
        pltpu.make_async_copy(source, target, load_sem.at[index])
        for index, (source, target) in enumerate(
            (
                (q_hbm, q_ref),
                (k_hbm, k_ref),
                (v_hbm, vbuf.at[me]),
                (tiles_hbm, tiles_ref),
                (gq_hbm, gq_ref),
                (gk_hbm, gk_ref),
            )
        )
    ]
    for load in loads:
        load.start()

    side = 1 - 2 * lax.rem(me, 2)
    partner = me + side
    ahead = me + 2 * side
    behind = me - 2 * side

    def inside(index):
        return jnp.logical_and(index >= 0, index < frames)

    barrier = pltpu.get_barrier_semaphore()
    pl.semaphore_signal(barrier, inc=1, device_id={"frame": partner}, device_id_type=MESH)
    for other in (me + 2, me - 2):

        @pl.when(inside(other))
        def _():
            pl.semaphore_signal(barrier, inc=1, device_id={"frame": other}, device_id_type=MESH)

    for step in range(1, tensors):
        pl.semaphore_signal(
            barrier, inc=1, device_id={"tensor": lax.rem(tpos + step, tensors)}, device_id_type=MESH
        )
    neighbours = inside(me + 2).astype(jnp.int32) + inside(me - 2).astype(jnp.int32)
    pl.semaphore_wait(barrier, neighbours + tensors)

    HEAD, FRONT, BACK = (0, BLK), (0, half), (half, rows - half)
    ACROSS, UP, DOWN = 0, 1, 2
    channels = {
        "k": (kbuf, kbuf.at[me], send_k, recv_k),
        "v": (vbuf, v_hbm, send_v, recv_v),
    }

    def copy(kind, origin, piece, dest, way, own=False):
        buf, own_ref, send, recv = channels[kind]
        part = int(piece is BACK)
        window = pl.ds(piece[0], piece[1])
        return pltpu.make_async_remote_copy(
            src_ref=own_ref.at[window] if own else buf.at[origin, window],
            dst_ref=buf.at[origin, window],
            send_sem=send.at[way, part, origin],
            recv_sem=recv.at[part, origin],
            device_id={"frame": dest},
            device_id_type=MESH,
        )

    def arrived(kind, origin, piece):
        buf, _, _, recv = channels[kind]
        view = buf.at[origin, pl.ds(piece[0], piece[1])]
        pltpu.make_async_copy(view, view, recv.at[int(piece is BACK), origin]).wait()

    def own_sends(kind, act):
        for first, second in ((FRONT, BACK), (BACK, FRONT)):
            act(copy(kind, me, second, partner, ACROSS, own=True))
            for other, way in ((me + 2, UP), (me - 2, DOWN)):

                @pl.when(inside(other))
                def _():
                    act(copy(kind, me, first, other, way, own=True))

    def near_relays(kind, act, wait):
        if wait:
            arrived(kind, partner, BACK)

        @pl.when(inside(ahead))
        def _():
            act(copy(kind, partner, BACK, ahead, UP))
            if wait:
                arrived(kind, ahead, FRONT)
            act(copy(kind, ahead, FRONT, partner, ACROSS))

        @pl.when(inside(behind))
        def _():
            if wait:
                arrived(kind, behind, FRONT)
            act(copy(kind, behind, HEAD, partner, ACROSS))

        @pl.when(jnp.logical_and(inside(ahead), inside(behind)))
        def _():
            act(copy(kind, ahead, HEAD, behind, DOWN))
            act(copy(kind, behind, HEAD, ahead, UP))

    def far_relays(kind, hops, act, wait):
        for sign, way in ((1, DOWN), (-1, UP)):
            origin = me + 2 * hops * sign
            dest = me - 2 * sign

            @pl.when(inside(origin))
            def _():
                if wait:
                    arrived(kind, origin, HEAD)

                @pl.when(inside(dest))
                def _():
                    act(copy(kind, origin, HEAD, dest, way))

                act(copy(kind, origin, HEAD, partner, ACROSS))

    def start(descriptor):
        descriptor.start()

    def finish(descriptor):
        descriptor.wait_send()

    own_sends("v", start)

    def squares(ref):
        total = None
        for head in range(heads):
            wide = ref[:, head * HD : (head + 1) * HD].astype(jnp.float32)
            total = wide * wide if total is None else total + wide * wide
        return jnp.sum(jnp.transpose(total), axis=0, keepdims=True)

    loads[0].wait()
    loads[1].wait()
    sums[tpos] = jnp.concatenate(
        [squares(q_ref), squares(k_ref), jnp.zeros((6, rows), jnp.float32)], axis=0
    )

    def sums_copy(peer):
        return pltpu.make_async_remote_copy(
            src_ref=sums.at[tpos],
            dst_ref=sums.at[tpos],
            send_sem=send_s.at[peer],
            recv_sem=recv_s.at[tpos],
            device_id={"tensor": peer},
            device_id_type=MESH,
        )

    for step in range(1, tensors):
        sums_copy(lax.rem(tpos + step, tensors)).start()

    for load in loads[2:]:
        load.wait()
    for slot in range(slots):
        listed[slot : slot + 1, :] = jnp.concatenate(
            [
                jnp.full((1, BLK), tiles_ref[me * blocks + block, slot], jnp.int32)
                for block in range(blocks)
            ],
            axis=1,
        )

    for step in range(1, tensors):
        peer = lax.rem(tpos + step, tensors)
        pltpu.make_async_copy(sums.at[peer], sums.at[peer], recv_s.at[peer]).wait()
    total = sums[0]
    for other in range(1, tensors):
        total = total + sums[other]
    factor = lax.rsqrt(total / (width * tensors) + EPS)

    def normed(ref, row, gain, store):
        scale = jnp.transpose(jnp.broadcast_to(factor[row : row + 1], (HD, rows)))
        for head in range(heads):
            columns = slice(head * HD, (head + 1) * HD)
            wide = ref[:, columns].astype(jnp.float32)
            store(columns, (wide * scale * gain[:, columns]).astype(jnp.bfloat16))

    def store_k(columns, value):
        kbuf[me, :, columns] = value

    def store_q(columns, value):
        qn[:, columns] = value

    normed(k_ref, 1, gk_ref[...].reshape(1, width), store_k)
    own_sends("k", start)
    normed(q_ref, 0, gq_ref[...].reshape(1, width), store_q)

    acc_ref[...] = jnp.zeros_like(acc_ref)
    max_ref[...] = jnp.full_like(max_ref, MASKED)
    sum_ref[...] = jnp.zeros_like(sum_ref)
    to_exponent = math.log2(math.e) / math.sqrt(HD)

    def attend(slab, keys, values):
        count = keys.shape[0] // BLK
        biases = []
        for block in range(count):
            hit = jnp.any(listed[0:slots, :] == slab * blocks + block, axis=0, keepdims=True)
            biases.append(jnp.where(hit, 0.0, MASKED))
        for head in range(heads):
            columns = slice(head * HD, (head + 1) * HD)
            scores = lax.dot_general(
                keys[:, columns],
                qn[:, columns],
                (((1,), (1,)), ((), ())),
                preferred_element_type=jnp.float32,
            )
            parts = [
                scores[block * BLK : (block + 1) * BLK] * to_exponent + biases[block]
                for block in range(count)
            ]
            top = functools.reduce(jnp.maximum, parts)
            old_max = max_ref[head : head + 1, :]
            new_max = jnp.maximum(old_max, jnp.max(top, axis=0, keepdims=True))
            shrink = jnp.exp2(old_max - new_max)
            weights = [jnp.exp2(part - new_max) for part in parts]
            added = functools.reduce(jnp.add, weights)
            max_ref[head : head + 1, :] = new_max
            sum_ref[head : head + 1, :] = sum_ref[head : head + 1, :] * shrink + jnp.sum(
                added, axis=0, keepdims=True
            )
            rounded = jnp.concatenate([weight.astype(jnp.bfloat16) for weight in weights], axis=0)
            product = lax.dot_general(
                values[:, columns],
                rounded,
                (((0,), (0,)), ((), ())),
                preferred_element_type=jnp.float32,
            )
            acc_ref[head] = acc_ref[head] * shrink + product

    last_hop = (frames - 1) // 2
    near_relays("v", start, True)
    attend(me, kbuf.at[me], vbuf.at[me])
    for hops in range(2, last_hop + 1):
        far_relays("v", hops, start, True)
    near_relays("k", start, True)

    arrived("v", partner, FRONT)
    arrived("k", partner, FRONT)
    attend(partner, kbuf.at[partner], vbuf.at[partner])

    def neighbour_step(other):
        @pl.when(inside(other))
        def _():
            arrived("v", other, BACK)
            arrived("k", other, BACK)
            attend(other, kbuf.at[other], vbuf.at[other])

    for hops in range(2, last_hop + 1):
        far_relays("k", hops, start, True)
    neighbour_step(ahead)
    neighbour_step(behind)

    @pl.loop(0, frames)
    def _(other):
        distance = jnp.abs(other - me)
        same_lane = lax.rem(distance, 2) == 0

        @pl.when(distance > NEAR)
        def _():
            @pl.when(jnp.logical_not(same_lane))
            def _():
                arrived("v", other, HEAD)
                arrived("k", other, HEAD)

            attend(other, kbuf.at[other, pl.ds(0, BLK)], vbuf.at[other, pl.ds(0, BLK)])

    diagonal = me - side

    @pl.when(inside(diagonal))
    def _():
        arrived("v", diagonal, FRONT)
        arrived("v", diagonal, BACK)
        arrived("k", diagonal, FRONT)
        arrived("k", diagonal, BACK)
        attend(diagonal, kbuf.at[diagonal], vbuf.at[diagonal])

    for head in range(heads):
        value = acc_ref[head] / sum_ref[head : head + 1, :]
        out_ref[:, head * HD : (head + 1) * HD] = jnp.transpose(value).astype(jnp.bfloat16)

    for kind in ("v", "k"):
        own_sends(kind, finish)
        near_relays(kind, finish, False)
        for hops in range(2, last_hop + 1):
            far_relays(kind, hops, finish, False)
    for step in range(1, tensors):
        sums_copy(lax.rem(tpos + step, tensors)).wait_send()


def body(frames, tensors, q_proj, k_proj, v_proj, gain_q, gain_k, tiles):
    rows, width = q_proj.shape
    heads = width // HD
    vmem = pl.BlockSpec(memory_space=pltpu.VMEM)
    slots = -(-tiles.shape[1] // 8) * 8
    return pl.pallas_call(
        functools.partial(kernel, frames, tensors),
        out_shape=jax.ShapeDtypeStruct((rows, width), jnp.bfloat16),
        in_specs=[pl.BlockSpec(memory_space=pltpu.HBM)] * 6,
        out_specs=vmem,
        scratch_shapes=[
            pltpu.SMEM(tiles.shape, jnp.int32),
            pltpu.VMEM((rows, width), jnp.bfloat16),
            pltpu.VMEM((rows, width), jnp.bfloat16),
            pltpu.VMEM((width,), jnp.float32),
            pltpu.VMEM((width,), jnp.float32),
            pltpu.VMEM((frames, rows, width), jnp.bfloat16),
            pltpu.VMEM((frames, rows, width), jnp.bfloat16),
            pltpu.VMEM((rows, width), jnp.bfloat16),
            pltpu.VMEM((tensors, 8, rows), jnp.float32),
            pltpu.VMEM((slots, rows), jnp.int32),
            pltpu.VMEM((heads, HD, rows), jnp.float32),
            pltpu.VMEM((8, rows), jnp.float32),
            pltpu.VMEM((8, rows), jnp.float32),
            pltpu.SemaphoreType.DMA((6,)),
            pltpu.SemaphoreType.DMA((3, 2, frames)),
            pltpu.SemaphoreType.DMA((3, 2, frames)),
            pltpu.SemaphoreType.DMA((2, frames)),
            pltpu.SemaphoreType.DMA((2, frames)),
            pltpu.SemaphoreType.DMA((tensors,)),
            pltpu.SemaphoreType.DMA((tensors,)),
        ],
        compiler_params=pltpu.CompilerParams(
            collective_id=0, has_side_effects=True, vmem_limit_bytes=40 * 1024 * 1024
        ),
    )(tiles, q_proj, k_proj, v_proj, gain_q, gain_k)


def solution(mesh):
    return jax.shard_map(
        functools.partial(body, mesh.shape["frame"], mesh.shape["tensor"]),
        mesh=mesh,
        in_specs=(
            P(("dp", "frame"), "tensor"),
            P(("dp", "frame"), "tensor"),
            P(("dp", "frame"), "tensor"),
            P("tensor"),
            P("tensor"),
            P("dp", None),
        ),
        out_specs=P(("dp", "frame"), "tensor"),
        check_vma=False,
    )
```

```python
import functools
import math

import jax
import jax.numpy as jnp
from jax import lax
from jax.experimental import pallas as pl
from jax.experimental.pallas import tpu as pltpu
from jax.sharding import PartitionSpec as P

HD = 128
BLK = 128
NEAR = 2
EPS = 1e-06
MASKED = -1e30
MESH = pl.DeviceIdType.MESH


def kernel(
    frames,
    tensors,
    tiles_hbm,
    q_hbm,
    k_hbm,
    v_hbm,
    gq_hbm,
    gk_hbm,
    out_ref,
    tiles_ref,
    q_ref,
    k_ref,
    gq_ref,
    gk_ref,
    kbuf,
    vbuf,
    qn,
    sums,
    listed,
    acc_ref,
    max_ref,
    sum_ref,
    load_sem,
    send_k,
    send_v,
    recv_k,
    recv_v,
    send_s,
    recv_s,
):
    me = lax.axis_index("frame")
    tpos = lax.axis_index("tensor")
    rows, width = q_ref.shape
    heads = width // HD
    blocks = rows // BLK
    slots = tiles_ref.shape[0]
    half = rows // 2

    loads = [
        pltpu.make_async_copy(source, target, load_sem.at[index])
        for index, (source, target) in enumerate(
            (
                (q_hbm, q_ref),
                (k_hbm, k_ref),
                (v_hbm, vbuf.at[me]),
                (tiles_hbm, tiles_ref),
                (gq_hbm, gq_ref),
                (gk_hbm, gk_ref),
            )
        )
    ]
    for load in loads:
        load.start()

    side = 1 - 2 * lax.rem(me, 2)
    partner = me + side
    ahead = me + 2 * side
    behind = me - 2 * side

    def inside(index):
        return jnp.logical_and(index >= 0, index < frames)

    barrier = pltpu.get_barrier_semaphore()
    pl.semaphore_signal(barrier, inc=1, device_id={"frame": partner}, device_id_type=MESH)
    for other in (me + 2, me - 2):

        @pl.when(inside(other))
        def _():
            pl.semaphore_signal(barrier, inc=1, device_id={"frame": other}, device_id_type=MESH)

    for step in range(1, tensors):
        pl.semaphore_signal(
            barrier, inc=1, device_id={"tensor": lax.rem(tpos + step, tensors)}, device_id_type=MESH
        )
    neighbours = inside(me + 2).astype(jnp.int32) + inside(me - 2).astype(jnp.int32)
    pl.semaphore_wait(barrier, neighbours + tensors)

    HEAD, FRONT, BACK = (0, BLK), (0, half), (half, rows - half)
    ACROSS, UP, DOWN = 0, 1, 2
    channels = {
        "k": (kbuf, kbuf.at[me], send_k, recv_k),
        "v": (vbuf, v_hbm, send_v, recv_v),
    }

    def copy(kind, origin, piece, dest, way, own=False):
        buf, own_ref, send, recv = channels[kind]
        part = int(piece is BACK)
        window = pl.ds(piece[0], piece[1])
        return pltpu.make_async_remote_copy(
            src_ref=own_ref.at[window] if own else buf.at[origin, window],
            dst_ref=buf.at[origin, window],
            send_sem=send.at[way, part, origin],
            recv_sem=recv.at[part, origin],
            device_id={"frame": dest},
            device_id_type=MESH,
        )

    def arrived(kind, origin, piece):
        buf, _, _, recv = channels[kind]
        view = buf.at[origin, pl.ds(piece[0], piece[1])]
        pltpu.make_async_copy(view, view, recv.at[int(piece is BACK), origin]).wait()

    def own_sends(kind, act):
        for first, second in ((FRONT, BACK), (BACK, FRONT)):
            act(copy(kind, me, second, partner, ACROSS, own=True))
            for other, way in ((me + 2, UP), (me - 2, DOWN)):

                @pl.when(inside(other))
                def _():
                    act(copy(kind, me, first, other, way, own=True))

    def near_relays(kind, act, wait):
        @pl.when(inside(ahead))
        def _():
            if wait:
                arrived(kind, ahead, FRONT)

        @pl.when(inside(behind))
        def _():
            if wait:
                arrived(kind, behind, FRONT)

        @pl.when(jnp.logical_and(inside(ahead), inside(behind)))
        def _():
            act(copy(kind, ahead, HEAD, behind, DOWN))
            act(copy(kind, behind, HEAD, ahead, UP))

        @pl.when(inside(behind))
        def _():
            act(copy(kind, behind, HEAD, partner, ACROSS))

        @pl.when(inside(ahead))
        def _():
            act(copy(kind, ahead, FRONT, partner, ACROSS))

        if wait:
            arrived(kind, partner, BACK)

        @pl.when(inside(ahead))
        def _():
            act(copy(kind, partner, BACK, ahead, UP))

    def far_relays(kind, hops, act, wait):
        for sign, way in ((1, DOWN), (-1, UP)):
            origin = me + 2 * hops * sign
            dest = me - 2 * sign

            @pl.when(inside(origin))
            def _():
                if wait:
                    arrived(kind, origin, HEAD)

                @pl.when(inside(dest))
                def _():
                    act(copy(kind, origin, HEAD, dest, way))

                act(copy(kind, origin, HEAD, partner, ACROSS))

    def start(descriptor):
        descriptor.start()

    def finish(descriptor):
        descriptor.wait_send()

    own_sends("v", start)

    def squares(ref):
        total = None
        for head in range(heads):
            wide = ref[:, head * HD : (head + 1) * HD].astype(jnp.float32)
            total = wide * wide if total is None else total + wide * wide
        return jnp.sum(jnp.transpose(total), axis=0, keepdims=True)

    loads[0].wait()
    loads[1].wait()
    sums[tpos] = jnp.concatenate(
        [squares(q_ref), squares(k_ref), jnp.zeros((6, rows), jnp.float32)], axis=0
    )

    def sums_copy(peer):
        return pltpu.make_async_remote_copy(
            src_ref=sums.at[tpos],
            dst_ref=sums.at[tpos],
            send_sem=send_s.at[peer],
            recv_sem=recv_s.at[tpos],
            device_id={"tensor": peer},
            device_id_type=MESH,
        )

    for step in range(1, tensors):
        sums_copy(lax.rem(tpos + step, tensors)).start()

    for load in loads[2:]:
        load.wait()
    for slot in range(slots):
        listed[slot : slot + 1, :] = jnp.concatenate(
            [
                jnp.full((1, BLK), tiles_ref[slot, me * blocks + block], jnp.int32)
                for block in range(blocks)
            ],
            axis=1,
        )

    for step in range(1, tensors):
        peer = lax.rem(tpos + step, tensors)
        pltpu.make_async_copy(sums.at[peer], sums.at[peer], recv_s.at[peer]).wait()
    total = sums[0]
    for other in range(1, tensors):
        total = total + sums[other]
    factor = lax.rsqrt(total / (width * tensors) + EPS)

    def normed(ref, row, gain, store):
        scale = jnp.transpose(jnp.broadcast_to(factor[row : row + 1], (HD, rows)))
        for head in range(heads):
            columns = slice(head * HD, (head + 1) * HD)
            wide = ref[:, columns].astype(jnp.float32)
            store(columns, (wide * scale * gain[:, columns]).astype(jnp.bfloat16))

    def store_k(columns, value):
        kbuf[me, :, columns] = value

    def store_q(columns, value):
        qn[:, columns] = value

    normed(k_ref, 1, gk_ref[...].reshape(1, width), store_k)
    own_sends("k", start)
    normed(q_ref, 0, gq_ref[...].reshape(1, width), store_q)

    acc_ref[...] = jnp.zeros_like(acc_ref)
    max_ref[...] = jnp.full_like(max_ref, MASKED)
    sum_ref[...] = jnp.zeros_like(sum_ref)
    to_exponent = math.log2(math.e) / math.sqrt(HD)

    def attend(slab, keys, values, first=0):
        count = keys.shape[0] // BLK
        biases = []
        for block in range(count):
            hit = jnp.any(listed[0:slots, :] == slab * blocks + first + block, axis=0, keepdims=True)
            biases.append(jnp.where(hit, 0.0, MASKED))
        for head in range(heads):
            columns = slice(head * HD, (head + 1) * HD)
            scores = lax.dot_general(
                keys[:, columns],
                qn[:, columns],
                (((1,), (1,)), ((), ())),
                preferred_element_type=jnp.float32,
            )
            parts = [
                scores[block * BLK : (block + 1) * BLK] * to_exponent + biases[block]
                for block in range(count)
            ]
            top = functools.reduce(jnp.maximum, parts)
            old_max = max_ref[head : head + 1, :]
            new_max = jnp.maximum(old_max, jnp.max(top, axis=0, keepdims=True))
            shrink = jnp.exp2(old_max - new_max)
            weights = [jnp.exp2(part - new_max) for part in parts]
            added = functools.reduce(jnp.add, weights)
            max_ref[head : head + 1, :] = new_max
            sum_ref[head : head + 1, :] = sum_ref[head : head + 1, :] * shrink + jnp.sum(
                added, axis=0, keepdims=True
            )
            rounded = jnp.concatenate([weight.astype(jnp.bfloat16) for weight in weights], axis=0)
            product = lax.dot_general(
                values[:, columns],
                rounded,
                (((0,), (0,)), ((), ())),
                preferred_element_type=jnp.float32,
            )
            acc_ref[head] = acc_ref[head] * shrink + product

    last_hop = (frames - 1) // 2
    near_relays("v", start, True)
    attend(me, kbuf.at[me], vbuf.at[me])
    for hops in range(2, last_hop + 1):
        far_relays("v", hops, start, True)
    near_relays("k", start, True)

    def neighbour_step(other):
        @pl.when(inside(other))
        def _():
            arrived("v", other, BACK)
            arrived("k", other, BACK)
            attend(other, kbuf.at[other], vbuf.at[other])

    def attend_head(other):
        attend(other, kbuf.at[other, pl.ds(0, BLK)], vbuf.at[other, pl.ds(0, BLK)])

    def partner_step():
        arrived("v", partner, FRONT)
        arrived("k", partner, FRONT)
        attend(partner, kbuf.at[partner], vbuf.at[partner])

    steps = [partner_step, lambda: neighbour_step(ahead), lambda: neighbour_step(behind)]
    for hops in range(2, last_hop + 1):
        if steps:
            steps.pop(0)()
        far_relays("k", hops, start, True)
    for step in steps:
        step()

    @pl.loop(2, last_hop + 1)
    def _(hops):
        for origin in (me + 2 * hops, me - 2 * hops):

            @pl.when(inside(origin))
            def _():
                attend_head(origin)

    diagonal = me - side

    @pl.when(inside(diagonal))
    def _():
        for piece in (FRONT, BACK):
            arrived("v", diagonal, piece)
            arrived("k", diagonal, piece)
            window = pl.ds(piece[0], piece[1])
            attend(
                diagonal,
                kbuf.at[diagonal, window],
                vbuf.at[diagonal, window],
                piece[0] // BLK,
            )

    @pl.loop(1, frames // 2)
    def _(index):
        distance = 2 * index + 1
        for origin in (me + distance, me - distance):

            @pl.when(inside(origin))
            def _():
                arrived("v", origin, HEAD)
                arrived("k", origin, HEAD)
                attend_head(origin)

    for head in range(heads):
        value = acc_ref[head] / sum_ref[head : head + 1, :]
        out_ref[:, head * HD : (head + 1) * HD] = jnp.transpose(value).astype(jnp.bfloat16)

    for kind in ("v", "k"):
        own_sends(kind, finish)
        near_relays(kind, finish, False)
        for hops in range(2, last_hop + 1):
            far_relays(kind, hops, finish, False)
    for step in range(1, tensors):
        sums_copy(lax.rem(tpos + step, tensors)).wait_send()


def body(frames, tensors, q_proj, k_proj, v_proj, gain_q, gain_k, tiles):
    rows, width = q_proj.shape
    heads = width // HD
    vmem = pl.BlockSpec(memory_space=pltpu.VMEM)
    slots = -(-tiles.shape[1] // 8) * 8
    return pl.pallas_call(
        functools.partial(kernel, frames, tensors),
        out_shape=jax.ShapeDtypeStruct((rows, width), jnp.bfloat16),
        in_specs=[pl.BlockSpec(memory_space=pltpu.HBM)] * 6,
        out_specs=vmem,
        scratch_shapes=[
            pltpu.SMEM(tiles.shape[::-1], jnp.int32),
            pltpu.VMEM((rows, width), jnp.bfloat16),
            pltpu.VMEM((rows, width), jnp.bfloat16),
            pltpu.VMEM((width,), jnp.float32),
            pltpu.VMEM((width,), jnp.float32),
            pltpu.VMEM((frames, rows, width), jnp.bfloat16),
            pltpu.VMEM((frames, rows, width), jnp.bfloat16),
            pltpu.VMEM((rows, width), jnp.bfloat16),
            pltpu.VMEM((tensors, 8, rows), jnp.float32),
            pltpu.VMEM((slots, rows), jnp.int32),
            pltpu.VMEM((heads, HD, rows), jnp.float32),
            pltpu.VMEM((8, rows), jnp.float32),
            pltpu.VMEM((8, rows), jnp.float32),
            pltpu.SemaphoreType.DMA((6,)),
            pltpu.SemaphoreType.DMA((3, 2, frames)),
            pltpu.SemaphoreType.DMA((3, 2, frames)),
            pltpu.SemaphoreType.DMA((2, frames)),
            pltpu.SemaphoreType.DMA((2, frames)),
            pltpu.SemaphoreType.DMA((tensors,)),
            pltpu.SemaphoreType.DMA((tensors,)),
        ],
        compiler_params=pltpu.CompilerParams(
            collective_id=0, has_side_effects=True, vmem_limit_bytes=63 * 1024 * 1024
        ),
    )(tiles.T, q_proj, k_proj, v_proj, gain_q, gain_k)


def solution(mesh):
    return jax.shard_map(
        functools.partial(body, mesh.shape["frame"], mesh.shape["tensor"]),
        mesh=mesh,
        in_specs=(
            P(("dp", "frame"), "tensor"),
            P(("dp", "frame"), "tensor"),
            P(("dp", "frame"), "tensor"),
            P("tensor"),
            P("tensor"),
            P("dp", None),
        ),
        out_specs=P(("dp", "frame"), "tensor"),
        check_vma=False,
    )
```

```python
import functools
import math

import jax
import jax.numpy as jnp
from jax import lax
from jax.experimental import pallas as pl
from jax.experimental.pallas import tpu as pltpu
from jax.sharding import PartitionSpec as P

HD = 128
BLK = 128
NEAR = 2
EPS = 1e-06
MASKED = -1e30
MESH = pl.DeviceIdType.MESH


def kernel(
    frames,
    tensors,
    tiles_hbm,
    q_hbm,
    k_hbm,
    v_hbm,
    gq_hbm,
    gk_hbm,
    out_ref,
    tiles_ref,
    q_ref,
    k_ref,
    gq_ref,
    gk_ref,
    kbuf,
    vbuf,
    qn,
    sums,
    listed,
    acc_ref,
    max_ref,
    sum_ref,
    load_sem,
    send_k,
    send_v,
    recv_k,
    recv_v,
    send_s,
    recv_s,
):
    me = lax.axis_index("frame")
    tpos = lax.axis_index("tensor")
    rows, width = q_ref.shape
    heads = width // HD
    blocks = rows // BLK
    slots = tiles_ref.shape[0]
    half = rows // 2

    loads = [
        pltpu.make_async_copy(source, target, load_sem.at[index])
        for index, (source, target) in enumerate(
            (
                (q_hbm, q_ref),
                (k_hbm, k_ref),
                (v_hbm, vbuf.at[me]),
                (tiles_hbm, tiles_ref),
                (gq_hbm, gq_ref),
                (gk_hbm, gk_ref),
            )
        )
    ]
    for load in loads:
        load.start()

    side = 1 - 2 * lax.rem(me, 2)
    partner = me + side
    ahead = me + 2 * side
    behind = me - 2 * side

    def inside(index):
        return jnp.logical_and(index >= 0, index < frames)

    barrier = pltpu.get_barrier_semaphore()
    pl.semaphore_signal(barrier, inc=1, device_id={"frame": partner}, device_id_type=MESH)
    for other in (me + 2, me - 2):

        @pl.when(inside(other))
        def _():
            pl.semaphore_signal(barrier, inc=1, device_id={"frame": other}, device_id_type=MESH)

    for step in range(1, tensors):
        pl.semaphore_signal(
            barrier, inc=1, device_id={"tensor": lax.rem(tpos + step, tensors)}, device_id_type=MESH
        )
    neighbours = inside(me + 2).astype(jnp.int32) + inside(me - 2).astype(jnp.int32)
    pl.semaphore_wait(barrier, neighbours + tensors)

    HEAD, FRONT, BACK = (0, BLK), (0, half), (half, rows - half)
    ACROSS, UP, DOWN = 0, 1, 2
    channels = {
        "k": (kbuf, kbuf.at[me], send_k, recv_k),
        "v": (vbuf, v_hbm, send_v, recv_v),
    }

    def copy(kind, origin, piece, dest, way, own=False):
        buf, own_ref, send, recv = channels[kind]
        part = int(piece is BACK)
        window = pl.ds(piece[0], piece[1])
        return pltpu.make_async_remote_copy(
            src_ref=own_ref.at[window] if own else buf.at[origin, window],
            dst_ref=buf.at[origin, window],
            send_sem=send.at[way, part, origin],
            recv_sem=recv.at[part, origin],
            device_id={"frame": dest},
            device_id_type=MESH,
        )

    def arrived(kind, origin, piece):
        buf, _, _, recv = channels[kind]
        view = buf.at[origin, pl.ds(piece[0], piece[1])]
        pltpu.make_async_copy(view, view, recv.at[int(piece is BACK), origin]).wait()

    def own_sends(kind, act):
        for first, second in ((FRONT, BACK), (BACK, FRONT)):
            act(copy(kind, me, second, partner, ACROSS, own=True))
            for other, way in ((me + 2, UP), (me - 2, DOWN)):

                @pl.when(inside(other))
                def _():
                    act(copy(kind, me, first, other, way, own=True))

    def head_relays(kind, act, wait):
        @pl.when(inside(ahead))
        def _():
            if wait:
                arrived(kind, ahead, FRONT)

        @pl.when(inside(behind))
        def _():
            if wait:
                arrived(kind, behind, FRONT)

        @pl.when(jnp.logical_and(inside(ahead), inside(behind)))
        def _():
            act(copy(kind, ahead, HEAD, behind, DOWN))
            act(copy(kind, behind, HEAD, ahead, UP))

        @pl.when(inside(behind))
        def _():
            act(copy(kind, behind, HEAD, partner, ACROSS))

    def diagonal_relays(kind, act):
        @pl.when(inside(ahead))
        def _():
            act(copy(kind, ahead, FRONT, partner, ACROSS))
            act(copy(kind, partner, BACK, ahead, UP))

    def far_relays(kind, hops, act, wait):
        for sign, way in ((1, DOWN), (-1, UP)):
            origin = me + 2 * hops * sign
            dest = me - 2 * sign

            @pl.when(inside(origin))
            def _():
                if wait:
                    arrived(kind, origin, HEAD)

                @pl.when(inside(dest))
                def _():
                    act(copy(kind, origin, HEAD, dest, way))

                act(copy(kind, origin, HEAD, partner, ACROSS))

    def start(descriptor):
        descriptor.start()

    def finish(descriptor):
        descriptor.wait_send()

    own_sends("v", start)

    def squares(ref):
        total = None
        for head in range(heads):
            wide = ref[:, head * HD : (head + 1) * HD].astype(jnp.float32)
            total = wide * wide if total is None else total + wide * wide
        return jnp.sum(jnp.transpose(total), axis=0, keepdims=True)

    loads[0].wait()
    loads[1].wait()
    sums[tpos] = jnp.concatenate(
        [squares(q_ref), squares(k_ref), jnp.zeros((6, rows), jnp.float32)], axis=0
    )

    def sums_copy(peer):
        return pltpu.make_async_remote_copy(
            src_ref=sums.at[tpos],
            dst_ref=sums.at[tpos],
            send_sem=send_s.at[peer],
            recv_sem=recv_s.at[tpos],
            device_id={"tensor": peer},
            device_id_type=MESH,
        )

    for step in range(1, tensors):
        sums_copy(lax.rem(tpos + step, tensors)).start()

    for load in loads[2:]:
        load.wait()
    for slot in range(slots):
        listed[slot : slot + 1, :] = jnp.concatenate(
            [
                jnp.full((1, BLK), tiles_ref[slot, me * blocks + block], jnp.int32)
                for block in range(blocks)
            ],
            axis=1,
        )

    for step in range(1, tensors):
        peer = lax.rem(tpos + step, tensors)
        pltpu.make_async_copy(sums.at[peer], sums.at[peer], recv_s.at[peer]).wait()
    total = sums[0]
    for other in range(1, tensors):
        total = total + sums[other]
    factor = lax.rsqrt(total / (width * tensors) + EPS)

    def normed(ref, row, gain, store):
        scale = jnp.transpose(jnp.broadcast_to(factor[row : row + 1], (HD, rows)))
        for head in range(heads):
            columns = slice(head * HD, (head + 1) * HD)
            wide = ref[:, columns].astype(jnp.float32)
            store(columns, (wide * scale * gain[:, columns]).astype(jnp.bfloat16))

    def store_k(columns, value):
        kbuf[me, :, columns] = value

    def store_q(columns, value):
        qn[:, columns] = value

    normed(k_ref, 1, gk_ref[...].reshape(1, width), store_k)
    own_sends("k", start)
    normed(q_ref, 0, gq_ref[...].reshape(1, width), store_q)

    acc_ref[...] = jnp.zeros_like(acc_ref)
    max_ref[...] = jnp.full_like(max_ref, MASKED)
    sum_ref[...] = jnp.zeros_like(sum_ref)
    to_exponent = math.log2(math.e) / math.sqrt(HD)

    def attend(slab, keys, values, first=0):
        count = keys.shape[0] // BLK
        biases = []
        for block in range(count):
            hit = jnp.any(listed[0:slots, :] == slab * blocks + first + block, axis=0, keepdims=True)
            biases.append(jnp.where(hit, 0.0, MASKED))
        for head in range(heads):
            columns = slice(head * HD, (head + 1) * HD)
            scores = lax.dot_general(
                keys[:, columns],
                qn[:, columns],
                (((1,), (1,)), ((), ())),
                preferred_element_type=jnp.float32,
            )
            parts = [
                scores[block * BLK : (block + 1) * BLK] * to_exponent + biases[block]
                for block in range(count)
            ]
            top = functools.reduce(jnp.maximum, parts)
            old_max = max_ref[head : head + 1, :]
            new_max = jnp.maximum(old_max, jnp.max(top, axis=0, keepdims=True))
            shrink = jnp.exp2(old_max - new_max)
            weights = [jnp.exp2(part - new_max) for part in parts]
            added = functools.reduce(jnp.add, weights)
            max_ref[head : head + 1, :] = new_max
            sum_ref[head : head + 1, :] = sum_ref[head : head + 1, :] * shrink + jnp.sum(
                added, axis=0, keepdims=True
            )
            rounded = jnp.concatenate([weight.astype(jnp.bfloat16) for weight in weights], axis=0)
            product = lax.dot_general(
                values[:, columns],
                rounded,
                (((0,), (0,)), ((), ())),
                preferred_element_type=jnp.float32,
            )
            acc_ref[head] = acc_ref[head] * shrink + product

    last_hop = (frames - 1) // 2
    head_relays("v", start, True)
    attend(me, kbuf.at[me], vbuf.at[me])
    head_relays("k", start, True)

    def neighbour_step(other):
        @pl.when(inside(other))
        def _():
            arrived("v", other, BACK)
            arrived("k", other, BACK)
            attend(other, kbuf.at[other], vbuf.at[other])

    def attend_head(other):
        attend(other, kbuf.at[other, pl.ds(0, BLK)], vbuf.at[other, pl.ds(0, BLK)])

    def partner_step():
        for piece in (BACK, FRONT):
            arrived("v", partner, piece)
            arrived("k", partner, piece)
        attend(partner, kbuf.at[partner], vbuf.at[partner])

    partner_step()
    diagonal_relays("v", start)
    if last_hop >= 2:
        far_relays("v", 2, start, True)
        far_relays("k", 2, start, True)
    diagonal_relays("k", start)
    neighbour_step(ahead)
    neighbour_step(behind)
    for hops in range(3, last_hop + 1):
        far_relays("v", hops, start, True)
        far_relays("k", hops, start, True)

    @pl.loop(2, last_hop + 1)
    def _(hops):
        for origin in (me + 2 * hops, me - 2 * hops):

            @pl.when(inside(origin))
            def _():
                attend_head(origin)

    @pl.loop(1, frames // 2)
    def _(index):
        distance = 2 * index + 1
        for origin in (me + distance, me - distance):

            @pl.when(inside(origin))
            def _():
                arrived("v", origin, HEAD)
                arrived("k", origin, HEAD)
                attend_head(origin)

    diagonal = me - side

    @pl.when(inside(diagonal))
    def _():
        for piece in (FRONT, BACK):
            arrived("v", diagonal, piece)
            arrived("k", diagonal, piece)
            window = pl.ds(piece[0], piece[1])
            attend(
                diagonal,
                kbuf.at[diagonal, window],
                vbuf.at[diagonal, window],
                piece[0] // BLK,
            )

    for head in range(heads):
        value = acc_ref[head] / sum_ref[head : head + 1, :]
        out_ref[:, head * HD : (head + 1) * HD] = jnp.transpose(value).astype(jnp.bfloat16)

    for kind in ("v", "k"):
        own_sends(kind, finish)
        head_relays(kind, finish, False)
        diagonal_relays(kind, finish)
        for hops in range(2, last_hop + 1):
            far_relays(kind, hops, finish, False)
    for step in range(1, tensors):
        sums_copy(lax.rem(tpos + step, tensors)).wait_send()


def body(frames, tensors, q_proj, k_proj, v_proj, gain_q, gain_k, tiles):
    rows, width = q_proj.shape
    heads = width // HD
    vmem = pl.BlockSpec(memory_space=pltpu.VMEM)
    slots = -(-tiles.shape[1] // 8) * 8
    return pl.pallas_call(
        functools.partial(kernel, frames, tensors),
        out_shape=jax.ShapeDtypeStruct((rows, width), jnp.bfloat16),
        in_specs=[pl.BlockSpec(memory_space=pltpu.HBM)] * 6,
        out_specs=vmem,
        scratch_shapes=[
            pltpu.SMEM(tiles.shape[::-1], jnp.int32),
            pltpu.VMEM((rows, width), jnp.bfloat16),
            pltpu.VMEM((rows, width), jnp.bfloat16),
            pltpu.VMEM((width,), jnp.float32),
            pltpu.VMEM((width,), jnp.float32),
            pltpu.VMEM((frames, rows, width), jnp.bfloat16),
            pltpu.VMEM((frames, rows, width), jnp.bfloat16),
            pltpu.VMEM((rows, width), jnp.bfloat16),
            pltpu.VMEM((tensors, 8, rows), jnp.float32),
            pltpu.VMEM((slots, rows), jnp.int32),
            pltpu.VMEM((heads, HD, rows), jnp.float32),
            pltpu.VMEM((8, rows), jnp.float32),
            pltpu.VMEM((8, rows), jnp.float32),
            pltpu.SemaphoreType.DMA((6,)),
            pltpu.SemaphoreType.DMA((3, 2, frames)),
            pltpu.SemaphoreType.DMA((3, 2, frames)),
            pltpu.SemaphoreType.DMA((2, frames)),
            pltpu.SemaphoreType.DMA((2, frames)),
            pltpu.SemaphoreType.DMA((tensors,)),
            pltpu.SemaphoreType.DMA((tensors,)),
        ],
        compiler_params=pltpu.CompilerParams(
            collective_id=0, has_side_effects=True, vmem_limit_bytes=63 * 1024 * 1024
        ),
    )(tiles.T, q_proj, k_proj, v_proj, gain_q, gain_k)


def solution(mesh):
    return jax.shard_map(
        functools.partial(body, mesh.shape["frame"], mesh.shape["tensor"]),
        mesh=mesh,
        in_specs=(
            P(("dp", "frame"), "tensor"),
            P(("dp", "frame"), "tensor"),
            P(("dp", "frame"), "tensor"),
            P("tensor"),
            P("tensor"),
            P("dp", None),
        ),
        out_specs=P(("dp", "frame"), "tensor"),
        check_vma=False,
    )
```
